32 devices in a mesh: expert: 8 (over y, x, core), dp: 4 (over z).
Axes of the slice: x: 2, y: 2, z: 4, core: 2. Of those that a mesh axis runs over, the one named last changes fastest.
Arguments:
- hidden: bfloat16 [4, 1024, 768], P('dp', 'expert'), may hold values from -6 to 6
- cotangent: bfloat16 [4, 1024, 768], P('dp', 'expert'), may hold values from -6 to 6
- norm1_gain: float32 [768], replicated, may hold values from 0.5 to 1.5
- w_query: bfloat16 [768, 768], P('dp'), may hold values from -0.21875 to 0.21875
- w_key: bfloat16 [768, 768], P('dp'), may hold values from -0.21875 to 0.21875
- w_value: bfloat16 [768, 768], P('dp'), may hold values from -0.21875 to 0.21875
- w_output: bfloat16 [768, 768], P('dp'), may hold values from -1.25 to 1.25
- bias_table: float32 [32, 12], replicated, may hold values from -6 to 6
- norm2_gain: float32 [768], replicated, may hold values from 0.5 to 1.5
- w_router: bfloat16 [768, 8], P('dp'), may hold values from -0.15625 to 0.15625
- w_in: bfloat16 [8, 768, 3072], P('expert', 'dp'), may hold values from -0.21875 to 0.21875
- w_out: bfloat16 [8, 3072, 768], P('expert', None, 'dp'), may hold values from -0.109375 to 0.109375
- expert_ids: int32 [4, 1024, 2], P('dp', 'expert'), may hold values from 0 to 7, all different within a row; in each aligned block of 128 rows (0 to 127, 128 to 255, ..., all dimensions but the last counted through in order) at most 36 rows name the same one
- keep_mask: int32 [4, 1024, 2], P('dp', 'expert'), may hold values 0 or 1
- buckets: int32 [1024], replicated, may hold values from 0 to 31
Outputs:
- output: bfloat16 [4, 1024, 768], P('dp', 'expert')
- grad_hidden: float32 [4, 1024, 768], P('dp', 'expert')
- grad_norm1_gain: float32 [768], P('dp')
- grad_w_query: float32 [768, 768], P('dp')
- grad_w_key: float32 [768, 768], P('dp')
- grad_w_value: float32 [768, 768], P('dp')
- grad_w_output: float32 [768, 768], P('dp')
- grad_bias_table: float32 [32, 12], P('dp')
- grad_norm2_gain: float32 [768], P('dp')
- grad_w_router: float32 [768, 8], P('dp')
- grad_w_in: float32 [8, 768, 3072], P('expert', 'dp')
- grad_w_out: float32 [8, 3072, 768], P('expert', None, 'dp')
The draws below stay inside these ranges and needn't reach their ends.
Inputs may be any that keep to these rules, and one draw needn't show every extreme that they name: `expert_ids`: each position names two different experts. Among the positions of one device (aligned blocks of 128 positions of a sequence) no expert is named more than 36 times, and in some blocks one is named exactly 36 times.
All inputs are finite; a program needn't handle non-finite values. No bound on the sum of `keep_mask` on one device may be relied on, other than what follows from the above.
Results may differ from the reference program's by a relative error of at most 0.013.
Values may be sent and summed in bfloat16 or wider, within the bound.
A program may use at most 256 MiB of HBM per device.

```python
import math
from functools import partial
import jax
import jax.numpy as jnp
import numpy as np
from jax import lax

D = 768
HEADS = 12
FF = 3072
NB = 32
TOK_DEV = 128
EXPERTS = 8
SEQS = 4
LENGTH = 1024
CAP = 36


def set_ends(entries, key, smallest, largest):
    place = [jax.random.randint(jax.random.fold_in(key, axis), (), 0, length) for axis, length in enumerate(entries.shape)]
    longest = entries.shape.index(max(entries.shape))
    beside = place[:longest] + [(place[longest] + 1) % entries.shape[longest]] + place[longest + 1:]
    return entries.at[tuple(place)].set(smallest).at[tuple(beside)].set(largest)


def steps_of(key, shape, split, smallest, top_value):
    gain, own = 1.0, jax.random.fold_in(key, 6)
    for axis_at, parts in split:
        steps = jnp.exp(jax.random.uniform(jax.random.fold_in(own, axis_at), (parts,), jnp.float32, smallest / len(split), top_value / len(split)))
        gain = gain * jnp.repeat(steps, shape[axis_at] // parts).reshape([-1 if axis == axis_at else 1 for axis in range(len(shape))])
    return gain


def assign_block(key, own, number, rows, amount, top, bound, skew):
    ranking = jax.random.permutation(key, amount)
    crowded, usual = load_shares(amount, rows * top, bound, skew, True), load_shares(amount, rows * top, bound, skew, False)
    places = jnp.arange(amount)

    def named(sizes, offset_by):
        used = int((sizes > 0).sum())
        fixed = max(1, used // 4)
        moved = fixed + (places - fixed + offset_by * (used - fixed)) % max(1, amount - fixed)
        return jnp.zeros((amount,), jnp.int32).at[ranking[jnp.where(places < fixed, places, moved)]].set(jnp.asarray(sizes, jnp.int32))

    sizes = jnp.where(number % 4 == 0, named(crowded, number // 4), named(usual, number - number // 4 - 1))
    mixed = jax.random.permutation(jax.random.fold_in(own, 3), amount)
    giver, sink = mixed[0:amount // 2 * 2:2], mixed[1:amount // 2 * 2:2]
    slack = jnp.minimum(sizes[giver] - 1, bound - sizes[sink]) // 2
    slack = jnp.where((giver == ranking[0]) | (sink == ranking[0]) | (sizes[sink] == 0), 0, jnp.maximum(slack, 0))
    moved = jax.random.randint(jax.random.fold_in(own, 4), (amount // 2,), 0, 1 << 20) % (slack + 1)
    sizes = sizes.at[giver].add(-moved).at[sink].add(moved)
    items = jnp.searchsorted(jnp.cumsum(sizes), jnp.arange(rows * top), side="right").astype(jnp.int32)
    listing = items.reshape(top, rows).T
    listing = listing[jax.random.permutation(jax.random.fold_in(own, 1), rows)]
    offset_by = jax.random.randint(jax.random.fold_in(own, 2), (rows, 1), 0, top)
    return jnp.take_along_axis(listing, (jnp.arange(top)[None, :] + offset_by) % top, axis=1)


def load_shares(number_of, total, limit, slope, full):
    portions = [(1 << 20) // math.isqrt(grade ** slope) + 1 for grade in range(1, number_of + 1)]
    largest = limit if full else min(limit, max(-(-total // number_of), total * portions[0] // sum(portions)))
    least = 1 if total - largest >= number_of - 1 else 0
    counts, surplus = [largest] + [least] * (number_of - 1), total - largest - least * (number_of - 1)
    while surplus > 0:
        movable = [i for i in range(1, number_of) if counts[i] < largest] or [i for i in range(1, number_of) if counts[i] < limit]
        whole, left = sum([portions[i] for i in movable]), surplus
        for i in movable:
            more = min(limit - counts[i], max(1, left * portions[i] // whole), surplus)
            counts[i] = counts[i] + more
            surplus = surplus - more
    return np.array(counts)


def normal_values(own_key, extent, scale, most, pieces=(), kind=jnp.bfloat16):
    loudness = steps_of(own_key, extent, pieces, -0.22, 0.18) if pieces else 1.0
    values = jax.random.normal(own_key, extent, jnp.float32) * scale * loudness
    return jnp.minimum(jnp.maximum(values, -most), most).astype(kind)


def setup_inputs(seed: int = 0) -> dict:
    key_list = jax.random.split(jax.random.key(seed), 16)
    hidden = normal_values(key_list[0], (SEQS, LENGTH, D), 1.0, 6.0, ((0, 4), (1, 8)))
    cotangent = normal_values(key_list[1], (SEQS, LENGTH, D), 1.0, 6.0, ((0, 4), (1, 8)))
    norm1_gain = jnp.clip(1.0 + 0.1 * jax.random.normal(key_list[2], (D,), jnp.float32), 0.5, 1.5)
    w_query = normal_values(key_list[3], (D, D), D ** -0.5, 0.21875, ((0, 4),))
    w_key = normal_values(key_list[4], (D, D), D ** -0.5, 0.21875, ((0, 4),))
    w_value = normal_values(key_list[5], (D, D), D ** -0.5, 0.21875, ((0, 4),))
    w_output = normal_values(key_list[6], (D, D), (D // 32) ** -0.5, 1.25, ((0, 4),))
    bias_table = normal_values(key_list[7], (NB, HEADS), 1.0, 6.0, (), jnp.float32)
    norm2_gain = jnp.clip(1.0 + 0.1 * jax.random.normal(key_list[8], (D,), jnp.float32), 0.5, 1.5)
    w_router = normal_values(key_list[9], (D, EXPERTS), (2 * D) ** -0.5, 0.15625, ((0, 4),))
    w_in = normal_values(key_list[10], (EXPERTS, D, FF), D ** -0.5, 0.21875, ((0, 8), (1, 4)))
    w_out = normal_values(key_list[11], (EXPERTS, FF, D), FF ** -0.5, 0.109375, ((0, 8), (2, 4)))
    expert_ids_keys = jax.random.split(jax.random.fold_in(key_list[12], 1), SEQS * LENGTH // TOK_DEV)
    expert_ids_turns = jax.random.permutation(jax.random.fold_in(key_list[12], 3), SEQS * LENGTH // TOK_DEV)
    expert_ids = jax.vmap(lambda own, number: assign_block(jax.random.fold_in(key_list[12], 2), own, number, TOK_DEV, EXPERTS, 2, CAP, 2))(expert_ids_keys, expert_ids_turns).reshape((SEQS, LENGTH, 2))
    keep_mask = set_ends((jax.random.randint(key_list[13], (SEQS, LENGTH, 2), 0, 8) < 7).astype(jnp.int32), jax.random.fold_in(key_list[13], 1), 0, 1)
    buckets = set_ends(jax.random.randint(key_list[14], (LENGTH,), 0, NB), jax.random.fold_in(key_list[14], 1), 0, NB - 1).astype(jnp.int32)
    return dict(hidden=hidden, cotangent=cotangent, norm1_gain=norm1_gain, w_query=w_query, w_key=w_key, w_value=w_value, w_output=w_output, bias_table=bias_table, norm2_gain=norm2_gain, w_router=w_router, w_in=w_in, w_out=w_out, expert_ids=expert_ids, keep_mask=keep_mask, buckets=buckets)


HIGHEST = lax.Precision.HIGHEST
NEGATIVE = -1e+30
EPSILON = 1e-06

@jax.custom_vjp
def low(v):
    return lax.optimization_barrier(v.astype(jnp.bfloat16)).astype(jnp.float32)

@jax.custom_vjp
def low_back(v):
    return v

def low_keep(v):
    return (low(v), None)

def low_pass(kept, grad):
    return (grad,)

def back_keep(v):
    return (v, None)

def back_low(kept, grad):
    return (low(grad),)
low.defvjp(low_keep, low_pass)
low_back.defvjp(back_keep, back_low)

def rms_norm(values, scale_gain):
    return values * lax.rsqrt(lax.optimization_barrier(jnp.mean(values * values, axis=-1, keepdims=True)) + EPSILON) * scale_gain

def slot_targets(expert_ids, keep_flags, experts, capacity):
    flat_ids = expert_ids.reshape(-1)
    flat_keep = keep_flags.reshape(-1)
    markers = (flat_ids[:, None] == jnp.arange(experts, dtype=jnp.int32)[None, :]).astype(jnp.int32) * flat_keep[:, None]
    earlier = jnp.cumsum(markers, axis=0) - markers
    places = lax.optimization_barrier(jnp.sum(earlier * markers, axis=1))
    return jnp.where(flat_keep > 0, flat_ids * capacity + places, experts * capacity).astype(jnp.int32)

def attention(queries, key_proj, value_proj, table, buckets):
    seq_count, seq_len, model_width = queries.shape
    head_count = table.shape[1]
    head_size = model_width // head_count
    block_size = min(512, seq_len)
    per_seq = seq_len // block_size
    query_blocks = queries.reshape(seq_count * per_seq, block_size, head_count, head_size)
    key_heads = key_proj.reshape(seq_count, seq_len, head_count, head_size)
    value_heads = value_proj.reshape(seq_count, seq_len, head_count, head_size)
    key_pos = jnp.arange(seq_len, dtype=jnp.int32)
    numbers = jnp.arange(seq_count * per_seq, dtype=jnp.int32)

    def one_block(inputs):
        query_block, number = inputs
        sequence = number // per_seq
        row_start = number % per_seq * block_size
        keys_here = lax.dynamic_index_in_dim(key_heads, sequence, 0, keepdims=False)
        values_here = lax.dynamic_index_in_dim(value_heads, sequence, 0, keepdims=False)
        raw_scores = jnp.einsum('qhd,khd->hqk', query_block, keys_here, precision=HIGHEST) * 0.125
        query_pos = row_start + jnp.arange(block_size, dtype=jnp.int32)
        offset = query_pos[:, None] - key_pos[None, :]
        bias_values = jnp.take(table, jnp.take(buckets, jnp.clip(offset, 0, seq_len - 1), axis=0), axis=0)
        scores = low_back(raw_scores + jnp.transpose(bias_values, (2, 0, 1)))
        scores = jnp.where((offset >= 0)[None], scores, NEGATIVE)
        weights = low(jax.nn.softmax(scores, axis=-1))
        return jnp.einsum('hqk,khd->qhd', weights, values_here, precision=HIGHEST)
    mixed = lax.map(jax.checkpoint(one_block), (query_blocks, numbers))
    return mixed.reshape(seq_count, seq_len, model_width)

def experts_apply(normed, gates, expert_ids, keep_mask, w_first, w_second):
    seq_count, seq_len, model_width = normed.shape
    expert_count = w_first.shape[0]
    sources = seq_len // TOK_DEV
    slotter = partial(slot_targets, experts=expert_count, capacity=CAP)
    targets = jax.vmap(jax.vmap(slotter))(expert_ids.reshape(seq_count, sources, TOK_DEV, 2), keep_mask.reshape(seq_count, sources, TOK_DEV, 2))
    owner = targets // CAP
    places = targets % CAP
    live = targets < expert_count * CAP
    seq_index = jnp.arange(seq_count, dtype=jnp.int32)[:, None, None]
    source_index = jnp.arange(sources, dtype=jnp.int32)[None, :, None]
    slots_all = expert_count * seq_count * sources * CAP
    where_to = jnp.where(live, ((owner * seq_count + seq_index) * sources + source_index) * CAP + places, slots_all).reshape(-1)
    spread = jnp.repeat(normed.reshape(seq_count, sources, TOK_DEV, model_width), 2, axis=2).reshape(-1, model_width)
    buffer = jnp.zeros((slots_all, model_width), jnp.float32).at[where_to].set(spread, mode='drop')
    buffer = low_back(buffer).reshape(expert_count, seq_count * sources * CAP, model_width)

    def one_expert(inputs):
        arrived, first_weight, second_weight = inputs
        pre_act = low_back(jnp.dot(arrived, first_weight, precision=HIGHEST))
        activated = low(jax.nn.gelu(pre_act, approximate=False))
        return low_back(low(jnp.dot(activated, second_weight, precision=HIGHEST)))
    expert_out = lax.map(jax.checkpoint(one_expert), (buffer, w_first, w_second)).reshape(-1, model_width)
    picked = jnp.take(expert_out, where_to, axis=0, mode='fill', fill_value=0.0).reshape(seq_count, seq_len, 2, model_width)
    return lax.optimization_barrier(jnp.sum(gates[:, :, :, None] * picked, axis=2))

def layer(inputs, gain_one, weight_query, weight_key, weight_value, weight_output, table, gain_two, weight_router, w_first, w_second, expert_ids, keep_mask, buckets):
    normed1 = low(rms_norm(inputs, gain_one))

    def project(weight):
        return low_back(low(jnp.einsum('bld,de->ble', normed1, weight, precision=HIGHEST)))
    mixed = attention(project(weight_query), project(weight_key), project(weight_value), table, buckets)
    attended = low_back(low(mixed))
    resid = inputs + low_back(jnp.einsum('bld,de->ble', attended, weight_output, precision=HIGHEST))
    normed2 = rms_norm(resid, gain_two)
    probs = jax.nn.softmax(jnp.einsum('bld,de->ble', normed2, weight_router, precision=HIGHEST), axis=-1)
    picked = jnp.take_along_axis(probs, expert_ids, axis=-1)
    gates = picked / lax.optimization_barrier(jnp.sum(picked, axis=-1, keepdims=True)) * keep_mask.astype(jnp.float32)
    return resid + experts_apply(low(normed2), gates, expert_ids, keep_mask, w_first, w_second)

def reference(hidden, cotangent, norm1_gain, w_query, w_key, w_value, w_output, bias_table, norm2_gain, w_router, w_in, w_out, expert_ids, keep_mask, buckets):
    forward = partial(layer, expert_ids=expert_ids, keep_mask=keep_mask, buckets=buckets)
    output, pullback = jax.vjp(forward, hidden.astype(jnp.float32), norm1_gain.astype(jnp.float32), w_query.astype(jnp.float32), w_key.astype(jnp.float32), w_value.astype(jnp.float32), w_output.astype(jnp.float32), bias_table.astype(jnp.float32), norm2_gain.astype(jnp.float32), w_router.astype(jnp.float32), w_in.astype(jnp.float32), w_out.astype(jnp.float32))
    grads = pullback(cotangent.astype(jnp.float32))
    return (output.astype(jnp.bfloat16), grads[0], grads[1], grads[2], grads[3], grads[4], grads[5], grads[6], grads[7], grads[8], grads[9], grads[10])
```

```python
from functools import partial

import jax
import jax.numpy as jnp
from jax import lax
from jax.experimental import pallas as pl
from jax.experimental.pallas import tpu as pltpu
from jax.sharding import PartitionSpec as P

HIGHEST = lax.Precision.HIGHEST
NEGATIVE = -1e30
EPSILON = 1e-06
LANES = 128
VMEM_BYTES = 56 * 1024 * 1024


def rms_norm(values, scale_gain):
    return (
        values * lax.rsqrt(jnp.mean(values * values, axis=-1, keepdims=True) + EPSILON) * scale_gain
    )


def dot_nt(left, right):
    return lax.dot_general(
        left, right, (((1,), (1,)), ((), ())), preferred_element_type=jnp.float32
    )


def dot_nn(left, right):
    return jnp.dot(left, right, preferred_element_type=jnp.float32)


def spread_diagonals(row, rows, cols):
    wide = jnp.broadcast_to(row, (rows, row.shape[1]))
    return pltpu.roll(wide, 0, 1, stride=1, stride_axis=0)[:, :cols]


def head_masks(half):
    lane = lax.broadcasted_iota(jnp.int32, (1, LANES), 1)
    first = lane < half
    return (first, (first.astype(jnp.bfloat16), 1 - first.astype(jnp.bfloat16)))


def attend_kernel(q_ref, k_ref, v_ref, line_ref, mixed_ref, exact_ref, log_ref):
    half = LANES // 2
    first, masks = head_masks(half)
    rows, seq_len = (q_ref.shape[0], k_ref.shape[0])
    queries, keys, values = (q_ref[...], k_ref[...], v_ref[...])
    outs = []
    for head in range(2):
        scores = dot_nt(queries * masks[head], keys) * 0.125
        scores = scores + spread_diagonals(line_ref[head : head + 1, :], rows, seq_len)
        top = jnp.max(scores, axis=1, keepdims=True)
        raised = jnp.exp(scores - top)
        total = jnp.sum(raised, axis=1, keepdims=True)
        weights = raised * (1.0 / total)
        upper = weights.astype(jnp.bfloat16)
        lower = (weights - upper.astype(jnp.float32)).astype(jnp.bfloat16)
        rounded = dot_nn(upper, values)
        outs.append((rounded, rounded + dot_nn(lower, values), top + jnp.log(total)))
    mixed_ref[...] = jnp.where(first, outs[0][0], outs[1][0]).astype(jnp.bfloat16)
    exact_ref[...] = jnp.where(first, outs[0][1], outs[1][1])
    log_ref[...] = jnp.where(first, outs[0][2], outs[1][2])


def query_grad_kernel(q_ref, k_ref, v_ref, line_ref, grad_ref, exact_ref, log_ref, dq_ref, diag_ref):
    half = LANES // 2
    first, masks = head_masks(half)
    rows, seq_len = (q_ref.shape[0], k_ref.shape[0])
    queries, keys, values, grads = (q_ref[...], k_ref[...], v_ref[...], grad_ref[...])
    products = grads.astype(jnp.float32) * exact_ref[...]
    flip = (
        lax.broadcasted_iota(jnp.int32, (rows, rows), 0)
        + lax.broadcasted_iota(jnp.int32, (rows, rows), 1)
        == rows - 1
    ).astype(jnp.bfloat16)
    outs = []
    for head in range(2):
        scores = dot_nt(queries * masks[head], keys) * 0.125
        scores = scores + spread_diagonals(line_ref[head : head + 1, :], rows, seq_len)
        place = head * half
        weights = jnp.exp(scores - log_ref[:, place : place + 1])
        row_dots = jnp.sum(
            jnp.where(first if head == 0 else ~first, products, 0.0), axis=1, keepdims=True
        )
        grad_weights = dot_nt(grads * masks[head], values)
        grad_scores = (weights * (grad_weights - row_dots)).astype(jnp.bfloat16)
        outs.append(dot_nn(grad_scores, keys) * 0.125)
        turned = jnp.concatenate(
            [dot_nn(flip, grad_scores), jnp.zeros((rows, rows), jnp.float32)], axis=1
        )
        lined = pltpu.roll(turned, 0, 1, stride=1, stride_axis=0)
        diag_ref[head : head + 1, :] = jnp.sum(lined, axis=0, keepdims=True)
    dq_ref[...] = jnp.where(first, outs[0], outs[1]).astype(jnp.bfloat16)


def key_grad_kernel(k_ref, v_ref, q_ref, grad_ref, line_ref, stat_ref, dk_ref, dv_ref):
    half = LANES // 2
    first, masks = head_masks(half)
    rows, seq_len = (k_ref.shape[0], q_ref.shape[0])
    queries, keys, values, grads = (q_ref[...], k_ref[...], v_ref[...], grad_ref[...])
    outs = []
    for head in range(2):
        scores = dot_nt(keys * masks[head], queries) * 0.125
        scores = scores + spread_diagonals(line_ref[head : head + 1, :], rows, seq_len)
        weights = jnp.exp(scores - stat_ref[head : head + 1, :])
        grad_weights = dot_nt(values * masks[head], grads)
        grad_scores = (weights * (grad_weights - stat_ref[2 + head : 3 + head, :])).astype(
            jnp.bfloat16
        )
        outs.append(
            (dot_nn(grad_scores, queries) * 0.125, dot_nn(weights.astype(jnp.bfloat16), grads))
        )
    dk_ref[...] = jnp.where(first, outs[0][0], outs[1][0]).astype(jnp.bfloat16)
    dv_ref[...] = jnp.where(first, outs[0][1], outs[1][1]).astype(jnp.bfloat16)


def columns(rows, shift):
    return pl.BlockSpec((rows, LANES), lambda pair: (0, pair + shift))


def planes(depth, width):
    return pl.BlockSpec((None, depth, width), lambda pair: (pair, 0, 0))


def pair_call(kernel, pairs, in_specs, out_specs, out_shape, cost):
    return pl.pallas_call(
        kernel,
        grid=(pairs,),
        in_specs=in_specs,
        out_specs=out_specs,
        out_shape=out_shape,
        cost_estimate=pl.CostEstimate(flops=cost, bytes_accessed=cost // 100, transcendentals=0),
        compiler_params=pltpu.CompilerParams(vmem_limit_bytes=VMEM_BYTES),
    )


def split_three(values):
    top = lax.reduce_precision(values, 8, 7)
    rest = values - top
    middle = lax.reduce_precision(rest, 8, 7)
    return jnp.concatenate([top, middle, rest - middle], axis=1).astype(jnp.bfloat16)


def on_device(
    hidden,
    cotangent,
    norm1_gain,
    w_query,
    w_key,
    w_value,
    w_output,
    bias_table,
    norm2_gain,
    w_router,
    w_in,
    w_out,
    expert_ids,
    keep_mask,
    buckets,
):
    tok_rows = hidden.shape[1]
    model_width = hidden.shape[2]
    head_count = bias_table.shape[1]
    head_size = model_width // head_count
    experts = w_router.shape[1]
    capacity = 9 * tok_rows // (4 * experts)
    seq_len = buckets.shape[0]
    pairs = model_width // LANES
    bucket_count = bias_table.shape[0]
    my_index = lax.axis_index("expert")
    query_start = my_index * tok_rows
    width = seq_len + tok_rows

    wqkv = jnp.concatenate([w_query, w_key, w_value], axis=1)
    wrest = jnp.concatenate(
        [w_output, jnp.pad(w_router, ((0, 0), (0, LANES - experts)))], axis=1
    )
    wqkv_all = lax.all_gather(wqkv, "dp", axis=0, tiled=True)
    wrest_all = lax.all_gather(wrest, "dp", axis=0, tiled=True)
    first_weight = lax.all_gather(w_in[0], "dp", axis=0, tiled=True)
    second_turned = lax.all_gather(w_out[0].T, "dp", axis=0, tiled=True)
    output_all = wrest_all[:, :model_width]
    router = wrest_all[:, model_width : model_width + experts].astype(jnp.float32)

    def filler(count):
        return jnp.full((count,), bucket_count, jnp.int32)

    falling = jnp.concatenate([filler(tok_rows + 1), buckets[::-1], filler(seq_len)])
    rising = jnp.concatenate([filler(seq_len), buckets, filler(tok_rows)])
    seen = lax.dynamic_slice_in_dim(falling, seq_len - query_start, width, 0)
    seen_sums = lax.dynamic_slice_in_dim(falling, seq_len - query_start + 1, width, 0)
    seen_turned = lax.dynamic_slice_in_dim(
        rising, seq_len - tok_rows - query_start, width, 0
    )

    def bias_line(numbers):
        turned = jnp.concatenate([numbers[tok_rows:], numbers[:tok_rows]])
        onehot = (
            jnp.arange(bucket_count, dtype=jnp.int32)[:, None] == turned[None, :]
        ).astype(jnp.float32)
        line = lax.dot_general(
            bias_table, onehot, (((0,), (0,)), ((), ())), precision=HIGHEST
        )
        line = jnp.where((turned < bucket_count)[None, :], line, NEGATIVE)
        return line.reshape(pairs, 2, width)

    line = bias_line(seen)
    line_turned = bias_line(seen_turned)

    inputs = hidden[0].astype(jnp.float32)
    normed1_f, norm1_back = jax.vjp(rms_norm, inputs, norm1_gain)
    normed1 = normed1_f.astype(jnp.bfloat16)
    projected = jnp.dot(normed1, wqkv_all, preferred_element_type=jnp.float32).astype(jnp.bfloat16)
    mixed_all = lax.all_gather(projected, "expert", axis=0, tiled=True)
    pair_cost = 2 * tok_rows * seq_len * model_width
    mixer_specs = [
        columns(tok_rows, 0),
        columns(seq_len, pairs),
        columns(seq_len, 2 * pairs),
        planes(2, width),
    ]
    wide_shape = jax.ShapeDtypeStruct((tok_rows, model_width), jnp.float32)
    low_shape = jax.ShapeDtypeStruct((tok_rows, model_width), jnp.bfloat16)
    attended, exact_out, log_wide = pair_call(
        attend_kernel,
        pairs,
        mixer_specs,
        [columns(tok_rows, 0)] * 3,
        [low_shape, wide_shape, wide_shape],
        3 * pair_cost,
    )(projected, mixed_all, mixed_all, line)
    resid = inputs + jnp.dot(attended, output_all, preferred_element_type=jnp.float32)
    chosen = (
        expert_ids[0][:, :, None] == jnp.arange(experts, dtype=jnp.int32)[None, None, :]
    ).astype(jnp.float32)
    kept = keep_mask[0].astype(jnp.float32)

    def route(resid_rows, gain_two, router_weight):
        normed = rms_norm(resid_rows, gain_two)
        probs = jax.nn.softmax(jnp.dot(normed, router_weight, precision=HIGHEST), axis=-1)
        picked = jnp.sum(probs[:, None, :] * chosen, axis=-1)
        return (normed, picked / jnp.sum(picked, axis=-1, keepdims=True) * kept)

    (normed2_f, gates), route_back = jax.vjp(route, resid, norm2_gain, router)
    normed2 = normed2_f.astype(jnp.bfloat16)
    grad_top = cotangent[0].astype(jnp.float32)
    grad_made = (gates[:, :, None] * grad_top[:, None, :]).astype(jnp.bfloat16)
    markers = chosen * kept[:, :, None]
    both = markers.reshape(tok_rows, 2 * experts).astype(jnp.bfloat16)
    row_number = jnp.arange(tok_rows, dtype=jnp.int32)
    before = (row_number[None, :] < row_number[:, None]).astype(jnp.bfloat16)
    counts = jnp.dot(before, both, preferred_element_type=jnp.float32).reshape(
        tok_rows, 2, experts
    )
    counts = counts + jnp.stack(
        [jnp.zeros((experts,), jnp.float32), jnp.sum(markers[:, 0, :], axis=0)]
    )
    places = jnp.sum(counts * markers, axis=-1).astype(jnp.int32)
    slots = experts * capacity
    targets = jnp.where(
        keep_mask[0] > 0, expert_ids[0] * capacity + places, slots
    )
    flat_targets = jnp.concatenate([targets[:, 0], targets[:, 1]])
    placing = (
        flat_targets[:, None] == jnp.arange(slots, dtype=jnp.int32)[None, :]
    ).astype(jnp.bfloat16)
    rows_out = jnp.concatenate(
        [
            jnp.concatenate([normed2, grad_made[:, 0]], axis=1),
            jnp.concatenate([normed2, grad_made[:, 1]], axis=1),
        ],
        axis=0,
    )
    outgoing = (
        lax.dot_general(
            placing, rows_out, (((0,), (0,)), ((), ())), preferred_element_type=jnp.float32
        )
        .astype(jnp.bfloat16)
        .reshape(experts, capacity, 2 * model_width)
    )
    received = lax.all_to_all(
        outgoing, "expert", split_axis=0, concat_axis=0, tiled=True
    ).reshape(slots, 2 * model_width)
    arrived = received[:, :model_width]
    grad_arrived = received[:, model_width:]
    pre_act = jnp.dot(arrived, first_weight, preferred_element_type=jnp.float32)
    normal_cdf = 0.5 * (1.0 + lax.erf(pre_act * (0.5**0.5)))
    activated = (pre_act * normal_cdf).astype(jnp.bfloat16)
    slope = normal_cdf + pre_act * (jnp.exp(-0.5 * pre_act * pre_act) * 0.3989422804014327)
    expert_out = dot_nt(activated, second_turned).astype(jnp.bfloat16)
    grad_act = jnp.dot(grad_arrived, second_turned, preferred_element_type=jnp.float32)
    grad_pre = (grad_act * slope).astype(jnp.bfloat16)
    grad_rows = dot_nt(grad_pre, first_weight).astype(jnp.bfloat16)
    returned = lax.all_to_all(
        jnp.concatenate([expert_out, grad_rows], axis=1).reshape(
            experts, capacity, 2 * model_width
        ),
        "expert",
        split_axis=0,
        concat_axis=0,
        tiled=True,
    ).reshape(slots, 2 * model_width)

    def outer(left, right):
        return lax.dot_general(
            left, right, (((0,), (0,)), ((), ())), preferred_element_type=jnp.float32
        )

    grad_first = outer(arrived, grad_pre).astype(jnp.bfloat16)
    grad_second = outer(grad_arrived, activated).astype(jnp.bfloat16)
    first_sum = lax.psum_scatter(grad_first, "dp", scatter_dimension=0, tiled=True)
    second_sum = lax.psum_scatter(grad_second, "dp", scatter_dimension=0, tiled=True)
    back = jnp.dot(placing, returned, preferred_element_type=jnp.float32).reshape(
        2, tok_rows, 2 * model_width
    )
    picked_rows = jnp.transpose(back[:, :, :model_width], (1, 0, 2))
    output = (resid + jnp.sum(gates[:, :, None] * picked_rows, axis=1)).astype(jnp.bfloat16)
    grad_gates = jnp.sum(picked_rows * grad_top[:, None, :], axis=-1)
    grad_normed2 = back[0, :, model_width:] + back[1, :, model_width:]
    grad_resid_norm, grad_gain_two, grad_router = route_back((grad_normed2, grad_gates))
    grad_resid = grad_top + grad_resid_norm
    grad_branch = grad_resid.astype(jnp.bfloat16)
    grad_attended = dot_nt(grad_branch, output_all).astype(jnp.bfloat16)
    row_dots = jnp.sum(
        (grad_attended.astype(jnp.float32) * exact_out).reshape(tok_rows, head_count, head_size),
        axis=2,
    )
    log_total = log_wide.reshape(tok_rows, head_count, head_size)[:, :, 0]
    stats = jnp.concatenate([split_three(log_total), split_three(row_dots)], axis=1)
    stats = jnp.pad(stats, ((0, 0), (0, LANES - stats.shape[1])))
    packed = jnp.concatenate([grad_attended, stats], axis=1)
    packed_all = lax.all_gather(packed, "expert", axis=0, tiled=True)
    grad_query_low, diagonals = pair_call(
        query_grad_kernel,
        pairs,
        mixer_specs + [columns(tok_rows, 0)] * 3,
        [columns(tok_rows, 0), planes(2, width)],
        [low_shape, jax.ShapeDtypeStruct((pairs, 2, width), jnp.float32)],
        5 * pair_cost,
    )(projected, mixed_all, mixed_all, line, grad_attended, exact_out, log_wide)
    grad_output = outer(attended, grad_branch).astype(jnp.bfloat16)
    output_sum = lax.psum_scatter(grad_output, "dp", scatter_dimension=0, tiled=True)
    stats_all = packed_all[:, model_width : model_width + 6 * head_count].astype(jnp.float32)
    stats_all = jnp.sum(stats_all.reshape(seq_len, 2, 3, pairs, 2), axis=2)
    stats_all = jnp.transpose(stats_all, (2, 1, 3, 0)).reshape(pairs, 4, seq_len)
    grad_keys, grad_values = pair_call(
        key_grad_kernel,
        pairs,
        [
            columns(tok_rows, pairs),
            columns(tok_rows, 2 * pairs),
            columns(seq_len, 0),
            columns(seq_len, 0),
            planes(2, width),
            planes(4, seq_len),
        ],
        [columns(tok_rows, 0)] * 2,
        [low_shape, low_shape],
        4 * pair_cost,
    )(projected, projected, mixed_all, packed_all, line_turned, stats_all)
    grads_low = jnp.concatenate([grad_query_low, grad_keys, grad_values], axis=1)
    grad_qkv = outer(normed1, grads_low).astype(jnp.bfloat16)
    qkv_sum = lax.psum_scatter(grad_qkv, "dp", scatter_dimension=0, tiled=True)
    grad_normed1 = dot_nt(grads_low, wqkv_all)
    grad_inputs, grad_gain_one = norm1_back(grad_normed1)
    grad_hidden = (grad_resid + grad_inputs)[None]
    onehot_sums = (
        jnp.arange(bucket_count, dtype=jnp.int32)[:, None] == seen_sums[None, :]
    ).astype(jnp.float32)
    grad_table = lax.dot_general(
        onehot_sums,
        diagonals.reshape(head_count, width),
        (((1,), (1,)), ((), ())),
        precision=HIGHEST,
    )
    small = jnp.concatenate(
        [grad_gain_one, grad_gain_two, grad_table.reshape(-1), grad_router.reshape(-1)]
    )
    small = lax.psum(small, ("dp", "expert"))
    matrix_sums = lax.psum(jnp.concatenate([qkv_sum, output_sum], axis=1), "expert").astype(
        jnp.float32
    )
    my_part = lax.axis_index("dp")
    part_count = model_width // w_query.shape[0]

    def mine(values):
        size = values.shape[0] // part_count
        return lax.dynamic_slice_in_dim(values, my_part * size, size, 0)

    table_end = 2 * model_width + bucket_count * head_count
    return (
        output[None],
        grad_hidden,
        mine(small[:model_width]),
        matrix_sums[:, :model_width],
        matrix_sums[:, model_width : 2 * model_width],
        matrix_sums[:, 2 * model_width : 3 * model_width],
        matrix_sums[:, 3 * model_width :],
        mine(small[2 * model_width : table_end].reshape(bucket_count, head_count)),
        mine(small[model_width : 2 * model_width]),
        mine(small[table_end:].reshape(model_width, experts)),
        first_sum.astype(jnp.float32)[None],
        second_sum.astype(jnp.float32).T[None],
    )


def solution(mesh):
    return jax.shard_map(
        on_device,
        mesh=mesh,
        in_specs=(
            P("dp", "expert", None),
            P("dp", "expert", None),
            P(),
            P("dp", None),
            P("dp", None),
            P("dp", None),
            P("dp", None),
            P(),
            P(),
            P("dp", None),
            P("expert", "dp", None),
            P("expert", None, "dp"),
            P("dp", "expert", None),
            P("dp", "expert", None),
            P(),
        ),
        out_specs=(
            P("dp", "expert", None),
            P("dp", "expert", None),
            P("dp"),
            P("dp", None),
            P("dp", None),
            P("dp", None),
            P("dp", None),
            P("dp", None),
            P("dp"),
            P("dp", None),
            P("expert", "dp", None),
            P("expert", None, "dp"),
        ),
        check_vma=False,
    )
```

```python
from functools import partial

import jax
import jax.numpy as jnp
from jax import lax
from jax.experimental import pallas as pl
from jax.experimental.pallas import tpu as pltpu
from jax.sharding import PartitionSpec as P

HIGHEST = lax.Precision.HIGHEST
NEGATIVE = -1e30
EPSILON = 1e-06
LANES = 128
VMEM_BYTES = 56 * 1024 * 1024


def rms_norm(values, scale_gain):
    return (
        values * lax.rsqrt(jnp.mean(values * values, axis=-1, keepdims=True) + EPSILON) * scale_gain
    )


def dot_nt(left, right):
    return lax.dot_general(
        left, right, (((1,), (1,)), ((), ())), preferred_element_type=jnp.float32
    )


def dot_nn(left, right):
    return jnp.dot(left, right, preferred_element_type=jnp.float32)


def spread_diagonals(row, rows, cols):
    wide = jnp.broadcast_to(row, (rows, row.shape[1]))
    return pltpu.roll(wide, 0, 1, stride=1, stride_axis=0)[:, :cols]


def head_masks(half):
    lane = lax.broadcasted_iota(jnp.int32, (1, LANES), 1)
    first = lane < half
    return (first, (first.astype(jnp.bfloat16), 1 - first.astype(jnp.bfloat16)))


def attend_kernel(q_ref, k_ref, v_ref, line_ref, mixed_ref, exact_ref, log_ref):
    half = LANES // 2
    first, masks = head_masks(half)
    rows, seq_len = (q_ref.shape[0], k_ref.shape[0])
    queries, keys, values = (q_ref[...], k_ref[...], v_ref[...])
    outs = []
    for head in range(2):
        scores = dot_nt(queries * masks[head], keys) * 0.125
        scores = scores + spread_diagonals(line_ref[head : head + 1, :], rows, seq_len)
        top = jnp.max(scores, axis=1, keepdims=True)
        raised = jnp.exp(scores - top)
        total = jnp.sum(raised, axis=1, keepdims=True)
        weights = raised * (1.0 / total)
        upper = weights.astype(jnp.bfloat16)
        lower = (weights - upper.astype(jnp.float32)).astype(jnp.bfloat16)
        rounded = dot_nn(upper, values)
        outs.append((rounded, rounded + dot_nn(lower, values), top + jnp.log(total)))
    mixed_ref[...] = jnp.where(first, outs[0][0], outs[1][0]).astype(jnp.bfloat16)
    exact_ref[...] = jnp.where(first, outs[0][1], outs[1][1])
    log_ref[...] = jnp.where(first, outs[0][2], outs[1][2])


def query_grad_kernel(q_ref, k_ref, v_ref, line_ref, grad_ref, exact_ref, log_ref, dq_ref, diag_ref):
    half = LANES // 2
    first, masks = head_masks(half)
    rows, seq_len = (q_ref.shape[0], k_ref.shape[0])
    queries, keys, values, grads = (q_ref[...], k_ref[...], v_ref[...], grad_ref[...])
    products = grads.astype(jnp.float32) * exact_ref[...]
    flip = (
        lax.broadcasted_iota(jnp.int32, (rows, rows), 0)
        + lax.broadcasted_iota(jnp.int32, (rows, rows), 1)
        == rows - 1
    ).astype(jnp.bfloat16)
    outs = []
    for head in range(2):
        scores = dot_nt(queries * masks[head], keys) * 0.125
        scores = scores + spread_diagonals(line_ref[head : head + 1, :], rows, seq_len)
        place = head * half
        weights = jnp.exp(scores - log_ref[:, place : place + 1])
        row_dots = jnp.sum(
            jnp.where(first if head == 0 else ~first, products, 0.0), axis=1, keepdims=True
        )
        grad_weights = dot_nt(grads * masks[head], values)
        grad_scores = (weights * (grad_weights - row_dots)).astype(jnp.bfloat16)
        outs.append(dot_nn(grad_scores, keys) * 0.125)
        turned = jnp.concatenate(
            [dot_nn(flip, grad_scores), jnp.zeros((rows, rows), jnp.float32)], axis=1
        )
        lined = pltpu.roll(turned, 0, 1, stride=1, stride_axis=0)
        diag_ref[head : head + 1, :] = jnp.sum(lined, axis=0, keepdims=True)
    dq_ref[...] = jnp.where(first, outs[0], outs[1]).astype(jnp.bfloat16)


def key_grad_kernel(k_ref, v_ref, q_ref, grad_ref, line_ref, stat_ref, dk_ref, dv_ref):
    half = LANES // 2
    first, masks = head_masks(half)
    rows, seq_len = (k_ref.shape[0], q_ref.shape[0])
    queries, keys, values, grads = (q_ref[...], k_ref[...], v_ref[...], grad_ref[...])
    outs = []
    for head in range(2):
        scores = dot_nt(keys * masks[head], queries) * 0.125
        scores = scores + spread_diagonals(line_ref[head : head + 1, :], rows, seq_len)
        weights = jnp.exp(scores - stat_ref[head : head + 1, :])
        grad_weights = dot_nt(values * masks[head], grads)
        grad_scores = (weights * (grad_weights - stat_ref[2 + head : 3 + head, :])).astype(
            jnp.bfloat16
        )
        outs.append(
            (dot_nn(grad_scores, queries) * 0.125, dot_nn(weights.astype(jnp.bfloat16), grads))
        )
    dk_ref[...] = jnp.where(first, outs[0][0], outs[1][0]).astype(jnp.bfloat16)
    dv_ref[...] = jnp.where(first, outs[0][1], outs[1][1]).astype(jnp.bfloat16)


def columns(rows, shift):
    return pl.BlockSpec((rows, LANES), lambda pair: (0, pair + shift))


def planes(depth, width):
    return pl.BlockSpec((None, depth, width), lambda pair: (pair, 0, 0))


def pair_call(kernel, pairs, in_specs, out_specs, out_shape, cost):
    return pl.pallas_call(
        kernel,
        grid=(pairs,),
        in_specs=in_specs,
        out_specs=out_specs,
        out_shape=out_shape,
        cost_estimate=pl.CostEstimate(flops=cost, bytes_accessed=cost // 100, transcendentals=0),
        compiler_params=pltpu.CompilerParams(vmem_limit_bytes=VMEM_BYTES),
    )


def ring_step(values, count):
    return lax.ppermute(values, "dp", [(part, (part + 1) % count) for part in range(count)])


def ring_blocks(block, count):
    blocks = [block]
    for _ in range(count - 1):
        blocks.append(ring_step(blocks[-1], count))
    return blocks


def ring_sum(term, count):
    running = term(1).astype(jnp.bfloat16) if count > 1 else None
    for place in range(2, count):
        arrived = ring_step(running, count).astype(jnp.float32)
        running = (arrived + term(place)).astype(jnp.bfloat16)
    if count == 1:
        return term(0)
    return ring_step(running, count).astype(jnp.float32) + term(0)


def split_three(values):
    top = lax.reduce_precision(values, 8, 7)
    rest = values - top
    middle = lax.reduce_precision(rest, 8, 7)
    return jnp.concatenate([top, middle, rest - middle], axis=1).astype(jnp.bfloat16)


def on_device(
    hidden,
    cotangent,
    norm1_gain,
    w_query,
    w_key,
    w_value,
    w_output,
    bias_table,
    norm2_gain,
    w_router,
    w_in,
    w_out,
    expert_ids,
    keep_mask,
    buckets,
):
    tok_rows = hidden.shape[1]
    model_width = hidden.shape[2]
    head_count = bias_table.shape[1]
    head_size = model_width // head_count
    experts = w_router.shape[1]
    capacity = 9 * tok_rows // (4 * experts)
    seq_len = buckets.shape[0]
    pairs = model_width // LANES
    bucket_count = bias_table.shape[0]
    my_index = lax.axis_index("expert")
    query_start = my_index * tok_rows
    width = seq_len + tok_rows

    part_rows = w_query.shape[0]
    part_count = model_width // part_rows
    my_part = lax.axis_index("dp")
    lines = lax.axis_size("expert")
    share = part_rows // lines
    first_blocks = ring_blocks(w_in[0], part_count)
    second_blocks = ring_blocks(w_out[0].T, part_count)
    first_weight = jnp.concatenate(first_blocks, axis=0)
    second_turned = jnp.concatenate(second_blocks, axis=0)

    def my_share(matrix):
        return lax.dynamic_slice_in_dim(matrix, my_index * share, share, 0)

    mixer_share = jnp.concatenate(
        [
            my_share(w_query),
            my_share(w_key),
            my_share(w_value),
            my_share(w_output),
            jnp.pad(my_share(w_router), ((0, 0), (0, LANES - experts))),
        ],
        axis=1,
    )
    mixer_all = lax.all_gather(mixer_share, ("dp", "expert"), axis=0, tiled=True)
    wqkv_all = mixer_all[:, : 3 * model_width]
    output_all = mixer_all[:, 3 * model_width : 4 * model_width]
    router = mixer_all[:, 4 * model_width : 4 * model_width + experts].astype(jnp.float32)

    def turn(values):
        blocks = [
            values[:, part * part_rows : (part + 1) * part_rows]
            for part in range(part_count - 1, -1, -1)
        ]
        doubled = jnp.concatenate(blocks + blocks, axis=1)
        return lax.dynamic_slice_in_dim(
            doubled, (part_count - 1 - my_part) * part_rows, model_width, 1
        )

    def by_line(values):
        shaped = values.reshape(tok_rows, part_count, lines, share)
        return jnp.transpose(shaped, (0, 2, 1, 3)).reshape(tok_rows, model_width)

    def filler(count):
        return jnp.full((count,), bucket_count, jnp.int32)

    falling = jnp.concatenate([filler(tok_rows + 1), buckets[::-1], filler(seq_len)])
    rising = jnp.concatenate([filler(seq_len), buckets, filler(tok_rows)])
    seen = lax.dynamic_slice_in_dim(falling, seq_len - query_start, width, 0)
    seen_sums = lax.dynamic_slice_in_dim(falling, seq_len - query_start + 1, width, 0)
    seen_turned = lax.dynamic_slice_in_dim(
        rising, seq_len - tok_rows - query_start, width, 0
    )

    def bias_line(numbers):
        turned = jnp.concatenate([numbers[tok_rows:], numbers[:tok_rows]])
        onehot = (
            jnp.arange(bucket_count, dtype=jnp.int32)[:, None] == turned[None, :]
        ).astype(jnp.float32)
        line = lax.dot_general(
            bias_table, onehot, (((0,), (0,)), ((), ())), precision=HIGHEST
        )
        line = jnp.where((turned < bucket_count)[None, :], line, NEGATIVE)
        return line.reshape(pairs, 2, width)

    line = bias_line(seen)
    line_turned = bias_line(seen_turned)

    inputs = hidden[0].astype(jnp.float32)
    normed1_f, norm1_back = jax.vjp(rms_norm, inputs, norm1_gain)
    normed1 = normed1_f.astype(jnp.bfloat16)
    projected = jnp.dot(normed1, wqkv_all, preferred_element_type=jnp.float32).astype(jnp.bfloat16)
    mixed_all = lax.all_gather(projected[:, model_width:], "expert", axis=0, tiled=True)
    queries_all = lax.all_gather(projected[:, :model_width], "expert", axis=0, tiled=True)
    pair_cost = 2 * tok_rows * seq_len * model_width
    mixer_specs = [
        columns(tok_rows, 0),
        columns(seq_len, 0),
        columns(seq_len, pairs),
        planes(2, width),
    ]
    wide_shape = jax.ShapeDtypeStruct((tok_rows, model_width), jnp.float32)
    low_shape = jax.ShapeDtypeStruct((tok_rows, model_width), jnp.bfloat16)
    attended, exact_out, log_wide = pair_call(
        attend_kernel,
        pairs,
        mixer_specs,
        [columns(tok_rows, 0)] * 3,
        [low_shape, wide_shape, wide_shape],
        3 * pair_cost,
    )(projected, mixed_all, mixed_all, line)
    resid = inputs + jnp.dot(attended, output_all, preferred_element_type=jnp.float32)
    chosen = (
        expert_ids[0][:, :, None] == jnp.arange(experts, dtype=jnp.int32)[None, None, :]
    ).astype(jnp.float32)
    kept = keep_mask[0].astype(jnp.float32)

    def route(resid_rows, gain_two, router_weight):
        normed = rms_norm(resid_rows, gain_two)
        probs = jax.nn.softmax(jnp.dot(normed, router_weight, precision=HIGHEST), axis=-1)
        picked = jnp.sum(probs[:, None, :] * chosen, axis=-1)
        return (normed, picked / jnp.sum(picked, axis=-1, keepdims=True) * kept)

    (normed2_f, gates), route_back = jax.vjp(route, resid, norm2_gain, router)
    normed2 = normed2_f.astype(jnp.bfloat16)
    grad_top = cotangent[0].astype(jnp.float32)
    grad_turned = turn(cotangent[0]).astype(jnp.float32)
    grad_made = (gates[:, :, None] * grad_turned[:, None, :]).astype(jnp.bfloat16)
    normed_turned = turn(normed2)
    markers = chosen * kept[:, :, None]
    both = markers.reshape(tok_rows, 2 * experts).astype(jnp.bfloat16)
    row_number = jnp.arange(tok_rows, dtype=jnp.int32)
    before = (row_number[None, :] < row_number[:, None]).astype(jnp.bfloat16)
    counts = jnp.dot(before, both, preferred_element_type=jnp.float32).reshape(
        tok_rows, 2, experts
    )
    counts = counts + jnp.stack(
        [jnp.zeros((experts,), jnp.float32), jnp.sum(markers[:, 0, :], axis=0)]
    )
    places = jnp.sum(counts * markers, axis=-1).astype(jnp.int32)
    slots = experts * capacity
    targets = jnp.where(
        keep_mask[0] > 0, expert_ids[0] * capacity + places, slots
    )
    flat_targets = jnp.concatenate([targets[:, 0], targets[:, 1]])
    placing = (
        flat_targets[:, None] == jnp.arange(slots, dtype=jnp.int32)[None, :]
    ).astype(jnp.bfloat16)
    rows_out = jnp.concatenate(
        [
            jnp.concatenate([normed_turned, grad_made[:, 0]], axis=1),
            jnp.concatenate([normed_turned, grad_made[:, 1]], axis=1),
        ],
        axis=0,
    )
    outgoing = (
        lax.dot_general(
            placing, rows_out, (((0,), (0,)), ((), ())), preferred_element_type=jnp.float32
        )
        .astype(jnp.bfloat16)
        .reshape(experts, capacity, 2 * model_width)
    )
    received = lax.all_to_all(
        outgoing, "expert", split_axis=0, concat_axis=0, tiled=True
    ).reshape(slots, 2 * model_width)
    arrived = received[:, :model_width]
    grad_arrived = received[:, model_width:]
    pre_act = jnp.dot(arrived, first_weight, preferred_element_type=jnp.float32)
    normal_cdf = 0.5 * (1.0 + lax.erf(pre_act * (0.5**0.5)))
    activated = (pre_act * normal_cdf).astype(jnp.bfloat16)
    slope = normal_cdf + pre_act * (jnp.exp(-0.5 * pre_act * pre_act) * 0.3989422804014327)
    expert_out = dot_nt(activated, second_turned).astype(jnp.bfloat16)
    grad_act = jnp.dot(grad_arrived, second_turned, preferred_element_type=jnp.float32)
    grad_pre = (grad_act * slope).astype(jnp.bfloat16)
    grad_rows = dot_nt(grad_pre, first_weight).astype(jnp.bfloat16)
    returned = lax.all_to_all(
        jnp.concatenate([expert_out, grad_rows], axis=1).reshape(
            experts, capacity, 2 * model_width
        ),
        "expert",
        split_axis=0,
        concat_axis=0,
        tiled=True,
    ).reshape(slots, 2 * model_width)

    def outer(left, right):
        return lax.dot_general(
            left, right, (((0,), (0,)), ((), ())), preferred_element_type=jnp.float32
        )

    def feature_block(values, place):
        return values[:, place * part_rows : (place + 1) * part_rows]

    first_sum = ring_sum(lambda place: outer(feature_block(arrived, place), grad_pre), part_count)
    second_sum = ring_sum(
        lambda place: outer(feature_block(grad_arrived, place), activated), part_count
    )
    back = jnp.dot(placing, returned, preferred_element_type=jnp.float32).astype(jnp.bfloat16)
    made_back = turn(back[:, :model_width]).astype(jnp.float32)
    rows_back = turn(back[:, model_width:]).astype(jnp.float32)
    picked_rows = jnp.stack([made_back[:tok_rows], made_back[tok_rows:]], axis=1)
    output = (resid + jnp.sum(gates[:, :, None] * picked_rows, axis=1)).astype(jnp.bfloat16)
    grad_gates = jnp.sum(picked_rows * grad_top[:, None, :], axis=-1)
    grad_normed2 = rows_back[:tok_rows] + rows_back[tok_rows:]
    grad_resid_norm, grad_gain_two, grad_router = route_back((grad_normed2, grad_gates))
    grad_resid = grad_top + grad_resid_norm
    grad_branch = grad_resid.astype(jnp.bfloat16)
    grad_attended = dot_nt(grad_branch, output_all).astype(jnp.bfloat16)
    row_dots = jnp.sum(
        (grad_attended.astype(jnp.float32) * exact_out).reshape(tok_rows, head_count, head_size),
        axis=2,
    )
    log_total = log_wide.reshape(tok_rows, head_count, head_size)[:, :, 0]
    stats = jnp.concatenate([split_three(log_total), split_three(row_dots)], axis=1)
    stats = jnp.pad(stats, ((0, 0), (0, LANES - stats.shape[1])))
    packed = jnp.concatenate([grad_attended, stats], axis=1)
    packed_all = lax.all_gather(packed, "expert", axis=0, tiled=True)
    grad_query_low, diagonals = pair_call(
        query_grad_kernel,
        pairs,
        mixer_specs + [columns(tok_rows, 0)] * 3,
        [columns(tok_rows, 0), planes(2, width)],
        [low_shape, jax.ShapeDtypeStruct((pairs, 2, width), jnp.float32)],
        5 * pair_cost,
    )(projected, mixed_all, mixed_all, line, grad_attended, exact_out, log_wide)
    grad_output = outer(by_line(attended), grad_branch).astype(jnp.bfloat16)
    stats_all = packed_all[:, model_width : model_width + 6 * head_count].astype(jnp.float32)
    stats_all = jnp.sum(stats_all.reshape(seq_len, 2, 3, pairs, 2), axis=2)
    stats_all = jnp.transpose(stats_all, (2, 1, 3, 0)).reshape(pairs, 4, seq_len)
    grad_keys, grad_values = pair_call(
        key_grad_kernel,
        pairs,
        [
            columns(tok_rows, pairs),
            columns(tok_rows, 2 * pairs),
            columns(seq_len, 0),
            columns(seq_len, 0),
            planes(2, width),
            planes(4, seq_len),
        ],
        [columns(tok_rows, 0)] * 2,
        [low_shape, low_shape],
        4 * pair_cost,
    )(projected, projected, queries_all, packed_all, line_turned, stats_all)
    grads_low = jnp.concatenate([grad_query_low, grad_keys, grad_values], axis=1)
    grad_qkv = outer(by_line(normed1), grads_low).astype(jnp.bfloat16)
    grad_mixer = jnp.concatenate([grad_qkv, grad_output], axis=1)
    line_sum = lax.psum_scatter(grad_mixer, "expert", scatter_dimension=0, tiled=True)
    part_sum = lax.psum_scatter(line_sum, "dp", scatter_dimension=0, tiled=True)
    matrix_sums = lax.all_gather(part_sum, "expert", axis=0, tiled=True).astype(jnp.float32)
    grad_normed1 = dot_nt(grads_low, wqkv_all)
    grad_inputs, grad_gain_one = norm1_back(grad_normed1)
    grad_hidden = (grad_resid + grad_inputs)[None]
    onehot_sums = (
        jnp.arange(bucket_count, dtype=jnp.int32)[:, None] == seen_sums[None, :]
    ).astype(jnp.float32)
    grad_table = lax.dot_general(
        onehot_sums,
        diagonals.reshape(head_count, width),
        (((1,), (1,)), ((), ())),
        precision=HIGHEST,
    )
    small = jnp.concatenate(
        [grad_gain_one, grad_gain_two, grad_table.reshape(-1), grad_router.reshape(-1)]
    )
    small = lax.psum(small, ("dp", "expert"))

    def mine(values):
        size = values.shape[0] // part_count
        return lax.dynamic_slice_in_dim(values, my_part * size, size, 0)

    table_end = 2 * model_width + bucket_count * head_count
    return (
        output[None],
        grad_hidden,
        mine(small[:model_width]),
        matrix_sums[:, :model_width],
        matrix_sums[:, model_width : 2 * model_width],
        matrix_sums[:, 2 * model_width : 3 * model_width],
        matrix_sums[:, 3 * model_width :],
        mine(small[2 * model_width : table_end].reshape(bucket_count, head_count)),
        mine(small[model_width : 2 * model_width]),
        mine(small[table_end:].reshape(model_width, experts)),
        first_sum.astype(jnp.float32)[None],
        second_sum.astype(jnp.float32).T[None],
    )


def solution(mesh):
    return jax.shard_map(
        on_device,
        mesh=mesh,
        in_specs=(
            P("dp", "expert", None),
            P("dp", "expert", None),
            P(),
            P("dp", None),
            P("dp", None),
            P("dp", None),
            P("dp", None),
            P(),
            P(),
            P("dp", None),
            P("expert", "dp", None),
            P("expert", None, "dp"),
            P("dp", "expert", None),
            P("dp", "expert", None),
            P(),
        ),
        out_specs=(
            P("dp", "expert", None),
            P("dp", "expert", None),
            P("dp"),
            P("dp", None),
            P("dp", None),
            P("dp", None),
            P("dp", None),
            P("dp", None),
            P("dp"),
            P("dp", None),
            P("expert", "dp", None),
            P("expert", None, "dp"),
        ),
        check_vma=False,
    )
```

```python
from functools import partial

import jax
import jax.numpy as jnp
from jax import lax
from jax.experimental import pallas as pl
from jax.experimental.pallas import tpu as pltpu
from jax.sharding import PartitionSpec as P

HIGHEST = lax.Precision.HIGHEST
NEGATIVE = -1e30
EPSILON = 1e-06
LANES = 128
VMEM_BYTES = 56 * 1024 * 1024


def rms_norm(values, scale_gain):
    return (
        values * lax.rsqrt(jnp.mean(values * values, axis=-1, keepdims=True) + EPSILON) * scale_gain
    )


def dot_nt(left, right):
    return lax.dot_general(
        left, right, (((1,), (1,)), ((), ())), preferred_element_type=jnp.float32
    )


def dot_nn(left, right):
    return jnp.dot(left, right, preferred_element_type=jnp.float32)


def spread_diagonals(row, rows, cols):
    wide = jnp.broadcast_to(row, (rows, row.shape[1]))
    return pltpu.roll(wide, 0, 1, stride=1, stride_axis=0)[:, :cols]


def head_masks(half):
    lane = lax.broadcasted_iota(jnp.int32, (1, LANES), 1)
    first = lane < half
    return (first, (first.astype(jnp.bfloat16), 1 - first.astype(jnp.bfloat16)))


def attend_kernel(q_ref, k_ref, v_ref, line_ref, mixed_ref, exact_ref, log_ref):
    half = LANES // 2
    first, masks = head_masks(half)
    rows, seq_len = (q_ref.shape[0], k_ref.shape[0])
    queries, keys, values = (q_ref[...], k_ref[...], v_ref[...])
    outs = []
    for head in range(2):
        scores = dot_nt(queries * masks[head], keys) * 0.125
        scores = scores + spread_diagonals(line_ref[head : head + 1, :], rows, seq_len)
        top = jnp.max(scores, axis=1, keepdims=True)
        raised = jnp.exp(scores - top)
        total = jnp.sum(raised, axis=1, keepdims=True)
        weights = raised * (1.0 / total)
        upper = weights.astype(jnp.bfloat16)
        lower = (weights - upper.astype(jnp.float32)).astype(jnp.bfloat16)
        rounded = dot_nn(upper, values)
        outs.append((rounded, rounded + dot_nn(lower, values), top + jnp.log(total)))
    mixed_ref[...] = jnp.where(first, outs[0][0], outs[1][0]).astype(jnp.bfloat16)
    exact_ref[...] = jnp.where(first, outs[0][1], outs[1][1])
    log_ref[...] = jnp.where(first, outs[0][2], outs[1][2])


def query_grad_kernel(q_ref, k_ref, v_ref, line_ref, grad_ref, exact_ref, log_ref, dq_ref, diag_ref):
    half = LANES // 2
    first, masks = head_masks(half)
    rows, seq_len = (q_ref.shape[0], k_ref.shape[0])
    queries, keys, values, grads = (q_ref[...], k_ref[...], v_ref[...], grad_ref[...])
    products = grads.astype(jnp.float32) * exact_ref[...]
    flip = (
        lax.broadcasted_iota(jnp.int32, (rows, rows), 0)
        + lax.broadcasted_iota(jnp.int32, (rows, rows), 1)
        == rows - 1
    ).astype(jnp.bfloat16)
    outs = []
    for head in range(2):
        scores = dot_nt(queries * masks[head], keys) * 0.125
        scores = scores + spread_diagonals(line_ref[head : head + 1, :], rows, seq_len)
        place = head * half
        weights = jnp.exp(scores - log_ref[:, place : place + 1])
        row_dots = jnp.sum(
            jnp.where(first if head == 0 else ~first, products, 0.0), axis=1, keepdims=True
        )
        grad_weights = dot_nt(grads * masks[head], values)
        grad_scores = (weights * (grad_weights - row_dots)).astype(jnp.bfloat16)
        outs.append(dot_nn(grad_scores, keys) * 0.125)
        turned = jnp.concatenate(
            [dot_nn(flip, grad_scores), jnp.zeros((rows, rows), jnp.float32)], axis=1
        )
        lined = pltpu.roll(turned, 0, 1, stride=1, stride_axis=0)
        diag_ref[head : head + 1, :] = jnp.sum(lined, axis=0, keepdims=True)
    dq_ref[...] = jnp.where(first, outs[0], outs[1]).astype(jnp.bfloat16)


def key_grad_kernel(k_ref, v_ref, q_ref, grad_ref, line_ref, stat_ref, dk_ref, dv_ref):
    half = LANES // 2
    first, masks = head_masks(half)
    rows, seq_len = (k_ref.shape[0], q_ref.shape[0])
    queries, keys, values, grads = (q_ref[...], k_ref[...], v_ref[...], grad_ref[...])
    outs = []
    for head in range(2):
        scores = dot_nt(keys * masks[head], queries) * 0.125
        scores = scores + spread_diagonals(line_ref[head : head + 1, :], rows, seq_len)
        weights = jnp.exp(scores - stat_ref[head : head + 1, :])
        grad_weights = dot_nt(values * masks[head], grads)
        grad_scores = (weights * (grad_weights - stat_ref[2 + head : 3 + head, :])).astype(
            jnp.bfloat16
        )
        outs.append(
            (dot_nn(grad_scores, queries) * 0.125, dot_nn(weights.astype(jnp.bfloat16), grads))
        )
    dk_ref[...] = jnp.where(first, outs[0][0], outs[1][0]).astype(jnp.bfloat16)
    dv_ref[...] = jnp.where(first, outs[0][1], outs[1][1]).astype(jnp.bfloat16)


def columns(rows, shift):
    return pl.BlockSpec((rows, LANES), lambda pair: (0, pair + shift))


def planes(depth, width):
    return pl.BlockSpec((None, depth, width), lambda pair: (pair, 0, 0))


def pair_call(kernel, pairs, in_specs, out_specs, out_shape, cost):
    return pl.pallas_call(
        kernel,
        grid=(pairs,),
        in_specs=in_specs,
        out_specs=out_specs,
        out_shape=out_shape,
        cost_estimate=pl.CostEstimate(flops=cost, bytes_accessed=cost // 100, transcendentals=0),
        compiler_params=pltpu.CompilerParams(vmem_limit_bytes=VMEM_BYTES),
    )


def ring_step(values, count):
    return lax.ppermute(values, "dp", [(part, (part + 1) % count) for part in range(count)])


def ring_blocks(block, count):
    blocks = [block]
    for _ in range(count - 1):
        blocks.append(ring_step(blocks[-1], count))
    return blocks


def ring_hops(term, count):
    hops = [ring_step(term(1).astype(jnp.bfloat16), count)]
    for place in range(2, count):
        running = (hops[-1].astype(jnp.float32) + term(place)).astype(jnp.bfloat16)
        hops.append(ring_step(running, count))
    return hops


def split_three(values):
    top = lax.reduce_precision(values, 8, 7)
    rest = values - top
    middle = lax.reduce_precision(rest, 8, 7)
    return jnp.concatenate([top, middle, rest - middle], axis=1).astype(jnp.bfloat16)


def on_device(
    hidden,
    cotangent,
    norm1_gain,
    w_query,
    w_key,
    w_value,
    w_output,
    bias_table,
    norm2_gain,
    w_router,
    w_in,
    w_out,
    expert_ids,
    keep_mask,
    buckets,
):
    tok_rows = hidden.shape[1]
    model_width = hidden.shape[2]
    head_count = bias_table.shape[1]
    head_size = model_width // head_count
    experts = w_router.shape[1]
    capacity = 9 * tok_rows // (4 * experts)
    seq_len = buckets.shape[0]
    pairs = model_width // LANES
    bucket_count = bias_table.shape[0]
    my_index = lax.axis_index("expert")
    query_start = my_index * tok_rows
    width = seq_len + tok_rows

    part_rows = w_query.shape[0]
    part_count = model_width // part_rows
    my_part = lax.axis_index("dp")
    lines = lax.axis_size("expert")
    share = part_rows // lines
    first_blocks = ring_blocks(w_in[0], part_count)
    second_blocks = ring_blocks(w_out[0].T, part_count)

    def my_share(matrix):
        return lax.dynamic_slice_in_dim(matrix, my_index * share, share, 0)

    mixer_share = jnp.concatenate(
        [
            my_share(w_query),
            my_share(w_key),
            my_share(w_value),
            my_share(w_output),
            jnp.pad(my_share(w_router), ((0, 0), (0, LANES - experts))),
        ],
        axis=1,
    )
    mixer_all = lax.all_gather(mixer_share, ("dp", "expert"), axis=0, tiled=True)
    mixer_all, first_blocks[1], second_blocks[1] = lax.optimization_barrier(
        (mixer_all, first_blocks[1], second_blocks[1])
    )
    wqkv_all = mixer_all[:, : 3 * model_width]
    output_all = mixer_all[:, 3 * model_width : 4 * model_width]
    router = mixer_all[:, 4 * model_width : 4 * model_width + experts].astype(jnp.float32)

    def turn(values):
        blocks = [
            values[:, part * part_rows : (part + 1) * part_rows]
            for part in range(part_count - 1, -1, -1)
        ]
        doubled = jnp.concatenate(blocks + blocks, axis=1)
        return lax.dynamic_slice_in_dim(
            doubled, (part_count - 1 - my_part) * part_rows, model_width, 1
        )

    def by_line(values):
        shaped = values.reshape(tok_rows, part_count, lines, share)
        return jnp.transpose(shaped, (0, 2, 1, 3)).reshape(tok_rows, model_width)

    def filler(count):
        return jnp.full((count,), bucket_count, jnp.int32)

    falling = jnp.concatenate([filler(tok_rows + 1), buckets[::-1], filler(seq_len)])
    rising = jnp.concatenate([filler(seq_len), buckets, filler(tok_rows)])
    seen = lax.dynamic_slice_in_dim(falling, seq_len - query_start, width, 0)
    seen_sums = lax.dynamic_slice_in_dim(falling, seq_len - query_start + 1, width, 0)
    seen_turned = lax.dynamic_slice_in_dim(
        rising, seq_len - tok_rows - query_start, width, 0
    )

    def bias_line(numbers):
        turned = jnp.concatenate([numbers[tok_rows:], numbers[:tok_rows]])
        onehot = (
            jnp.arange(bucket_count, dtype=jnp.int32)[:, None] == turned[None, :]
        ).astype(jnp.float32)
        line = lax.dot_general(
            bias_table, onehot, (((0,), (0,)), ((), ())), precision=HIGHEST
        )
        line = jnp.where((turned < bucket_count)[None, :], line, NEGATIVE)
        return line.reshape(pairs, 2, width)

    line = bias_line(seen)
    line_turned = bias_line(seen_turned)

    inputs = hidden[0].astype(jnp.float32)
    normed1_f, norm1_back = jax.vjp(rms_norm, inputs, norm1_gain)
    normed1 = normed1_f.astype(jnp.bfloat16)
    projected = jnp.dot(normed1, wqkv_all, preferred_element_type=jnp.float32).astype(jnp.bfloat16)
    mixed_all = lax.all_gather(projected[:, model_width:], "expert", axis=0, tiled=True)
    mixed_all, first_blocks[2] = lax.optimization_barrier((mixed_all, first_blocks[2]))
    first_weight = jnp.concatenate(first_blocks, axis=0)
    second_turned = jnp.concatenate(second_blocks, axis=0)
    queries_all = lax.all_gather(projected[:, :model_width], "expert", axis=0, tiled=True)
    pair_cost = 2 * tok_rows * seq_len * model_width
    mixer_specs = [
        columns(tok_rows, 0),
        columns(seq_len, 0),
        columns(seq_len, pairs),
        planes(2, width),
    ]
    wide_shape = jax.ShapeDtypeStruct((tok_rows, model_width), jnp.float32)
    low_shape = jax.ShapeDtypeStruct((tok_rows, model_width), jnp.bfloat16)
    attended, exact_out, log_wide = pair_call(
        attend_kernel,
        pairs,
        mixer_specs,
        [columns(tok_rows, 0)] * 3,
        [low_shape, wide_shape, wide_shape],
        3 * pair_cost,
    )(projected, mixed_all, mixed_all, line)
    resid = inputs + jnp.dot(attended, output_all, preferred_element_type=jnp.float32)
    chosen = (
        expert_ids[0][:, :, None] == jnp.arange(experts, dtype=jnp.int32)[None, None, :]
    ).astype(jnp.float32)
    kept = keep_mask[0].astype(jnp.float32)

    def route(resid_rows, gain_two, router_weight):
        normed = rms_norm(resid_rows, gain_two)
        probs = jax.nn.softmax(jnp.dot(normed, router_weight, precision=HIGHEST), axis=-1)
        picked = jnp.sum(probs[:, None, :] * chosen, axis=-1)
        return (normed, picked / jnp.sum(picked, axis=-1, keepdims=True) * kept)

    (normed2_f, gates), route_back = jax.vjp(route, resid, norm2_gain, router)
    normed2 = normed2_f.astype(jnp.bfloat16)
    grad_top = cotangent[0].astype(jnp.float32)
    grad_turned = turn(cotangent[0]).astype(jnp.float32)
    grad_made = (gates[:, :, None] * grad_turned[:, None, :]).astype(jnp.bfloat16)
    normed_turned = turn(normed2)
    markers = chosen * kept[:, :, None]
    both = markers.reshape(tok_rows, 2 * experts).astype(jnp.bfloat16)
    row_number = jnp.arange(tok_rows, dtype=jnp.int32)
    before = (row_number[None, :] < row_number[:, None]).astype(jnp.bfloat16)
    counts = jnp.dot(before, both, preferred_element_type=jnp.float32).reshape(
        tok_rows, 2, experts
    )
    counts = counts + jnp.stack(
        [jnp.zeros((experts,), jnp.float32), jnp.sum(markers[:, 0, :], axis=0)]
    )
    places = jnp.sum(counts * markers, axis=-1).astype(jnp.int32)
    slots = experts * capacity
    targets = jnp.where(
        keep_mask[0] > 0, expert_ids[0] * capacity + places, slots
    )
    flat_targets = jnp.concatenate([targets[:, 0], targets[:, 1]])
    placing = (
        flat_targets[:, None] == jnp.arange(slots, dtype=jnp.int32)[None, :]
    ).astype(jnp.bfloat16)
    rows_out = jnp.concatenate(
        [
            jnp.concatenate([normed_turned, grad_made[:, 0]], axis=1),
            jnp.concatenate([normed_turned, grad_made[:, 1]], axis=1),
        ],
        axis=0,
    )
    outgoing = (
        lax.dot_general(
            placing, rows_out, (((0,), (0,)), ((), ())), preferred_element_type=jnp.float32
        )
        .astype(jnp.bfloat16)
        .reshape(experts, capacity, 2 * model_width)
    )
    received = lax.all_to_all(
        outgoing, "expert", split_axis=0, concat_axis=0, tiled=True
    ).reshape(slots, 2 * model_width)
    received, queries_all = lax.optimization_barrier((received, queries_all))
    arrived = received[:, :model_width]
    grad_arrived = received[:, model_width:]
    pre_act = jnp.dot(arrived, first_weight, preferred_element_type=jnp.float32)
    normal_cdf = 0.5 * (1.0 + lax.erf(pre_act * (0.5**0.5)))
    activated = (pre_act * normal_cdf).astype(jnp.bfloat16)
    slope = normal_cdf + pre_act * (jnp.exp(-0.5 * pre_act * pre_act) * 0.3989422804014327)
    expert_out = dot_nt(activated, second_turned).astype(jnp.bfloat16)
    grad_act = jnp.dot(grad_arrived, second_turned, preferred_element_type=jnp.float32)
    grad_pre = (grad_act * slope).astype(jnp.bfloat16)
    grad_rows = dot_nt(grad_pre, first_weight).astype(jnp.bfloat16)
    returned = lax.all_to_all(
        jnp.concatenate([expert_out, grad_rows], axis=1).reshape(
            experts, capacity, 2 * model_width
        ),
        "expert",
        split_axis=0,
        concat_axis=0,
        tiled=True,
    ).reshape(slots, 2 * model_width)

    def outer(left, right):
        return lax.dot_general(
            left, right, (((0,), (0,)), ((), ())), preferred_element_type=jnp.float32
        )

    def feature_block(values, place):
        return values[:, place * part_rows : (place + 1) * part_rows]

    def first_term(place):
        return outer(feature_block(arrived, place), grad_pre)

    def second_term(place):
        return outer(feature_block(grad_arrived, place), activated)

    first_hops = ring_hops(first_term, part_count)
    second_hops = ring_hops(second_term, part_count)
    back = jnp.dot(placing, returned, preferred_element_type=jnp.float32).astype(jnp.bfloat16)
    made_back = turn(back[:, :model_width]).astype(jnp.float32)
    rows_back = turn(back[:, model_width:]).astype(jnp.float32)
    picked_rows = jnp.stack([made_back[:tok_rows], made_back[tok_rows:]], axis=1)
    output = (resid + jnp.sum(gates[:, :, None] * picked_rows, axis=1)).astype(jnp.bfloat16)
    grad_gates = jnp.sum(picked_rows * grad_top[:, None, :], axis=-1)
    grad_normed2 = rows_back[:tok_rows] + rows_back[tok_rows:]
    grad_resid_norm, grad_gain_two, grad_router = route_back((grad_normed2, grad_gates))
    grad_resid = grad_top + grad_resid_norm
    grad_branch = grad_resid.astype(jnp.bfloat16)
    grad_attended = dot_nt(grad_branch, output_all).astype(jnp.bfloat16)
    row_dots = jnp.sum(
        (grad_attended.astype(jnp.float32) * exact_out).reshape(tok_rows, head_count, head_size),
        axis=2,
    )
    log_total = log_wide.reshape(tok_rows, head_count, head_size)[:, :, 0]
    stats = jnp.concatenate([split_three(log_total), split_three(row_dots)], axis=1)
    stats = jnp.pad(stats, ((0, 0), (0, LANES - stats.shape[1])))
    packed = jnp.concatenate([grad_attended, stats], axis=1)
    packed_all = lax.all_gather(packed, "expert", axis=0, tiled=True)
    packed_all, *_ = lax.optimization_barrier(
        (packed_all, first_hops[0], second_hops[0], first_hops[1])
    )
    grad_query_low, diagonals = pair_call(
        query_grad_kernel,
        pairs,
        mixer_specs + [columns(tok_rows, 0)] * 3,
        [columns(tok_rows, 0), planes(2, width)],
        [low_shape, jax.ShapeDtypeStruct((pairs, 2, width), jnp.float32)],
        5 * pair_cost,
    )(projected, mixed_all, mixed_all, line, grad_attended, exact_out, log_wide)
    grad_output = outer(by_line(attended), grad_branch).astype(jnp.bfloat16)
    stats_all = packed_all[:, model_width : model_width + 6 * head_count].astype(jnp.float32)
    stats_all = jnp.sum(stats_all.reshape(seq_len, 2, 3, pairs, 2), axis=2)
    stats_all = jnp.transpose(stats_all, (2, 1, 3, 0)).reshape(pairs, 4, seq_len)
    grad_keys, grad_values = pair_call(
        key_grad_kernel,
        pairs,
        [
            columns(tok_rows, pairs),
            columns(tok_rows, 2 * pairs),
            columns(seq_len, 0),
            columns(seq_len, 0),
            planes(2, width),
            planes(4, seq_len),
        ],
        [columns(tok_rows, 0)] * 2,
        [low_shape, low_shape],
        4 * pair_cost,
    )(projected, projected, queries_all, packed_all, line_turned, stats_all)
    grads_low = jnp.concatenate([grad_query_low, grad_keys, grad_values], axis=1)
    grad_qkv = outer(by_line(normed1), grads_low).astype(jnp.bfloat16)
    grad_normed1 = dot_nt(grads_low, wqkv_all)
    grad_inputs, grad_gain_one = norm1_back(grad_normed1)
    grad_hidden = (grad_resid + grad_inputs)[None]
    onehot_sums = (
        jnp.arange(bucket_count, dtype=jnp.int32)[:, None] == seen_sums[None, :]
    ).astype(jnp.float32)
    grad_table = lax.dot_general(
        onehot_sums,
        diagonals.reshape(head_count, width),
        (((1,), (1,)), ((), ())),
        precision=HIGHEST,
    )
    grad_mixer = jnp.concatenate([grad_qkv, grad_output], axis=1)
    line_sum = lax.psum_scatter(grad_mixer, "expert", scatter_dimension=0, tiled=True)
    small = jnp.concatenate(
        [grad_gain_one, grad_gain_two, grad_table.reshape(-1), grad_router.reshape(-1)]
    )
    small = lax.psum(small, ("dp", "expert"))
    line_sum, small = lax.optimization_barrier((line_sum, small))
    part_sum = lax.psum_scatter(line_sum, "dp", scatter_dimension=0, tiled=True)
    matrix_sums = lax.all_gather(part_sum, "expert", axis=0, tiled=True).astype(jnp.float32)
    first_sum = first_hops[-1].astype(jnp.float32) + first_term(0)
    second_sum = second_hops[-1].astype(jnp.float32) + second_term(0)

    def mine(values):
        size = values.shape[0] // part_count
        return lax.dynamic_slice_in_dim(values, my_part * size, size, 0)

    table_end = 2 * model_width + bucket_count * head_count
    return (
        output[None],
        grad_hidden,
        mine(small[:model_width]),
        matrix_sums[:, :model_width],
        matrix_sums[:, model_width : 2 * model_width],
        matrix_sums[:, 2 * model_width : 3 * model_width],
        matrix_sums[:, 3 * model_width :],
        mine(small[2 * model_width : table_end].reshape(bucket_count, head_count)),
        mine(small[model_width : 2 * model_width]),
        mine(small[table_end:].reshape(model_width, experts)),
        first_sum[None],
        second_sum.T[None],
    )


def solution(mesh):
    return jax.shard_map(
        on_device,
        mesh=mesh,
        in_specs=(
            P("dp", "expert", None),
            P("dp", "expert", None),
            P(),
            P("dp", None),
            P("dp", None),
            P("dp", None),
            P("dp", None),
            P(),
            P(),
            P("dp", None),
            P("expert", "dp", None),
            P("expert", None, "dp"),
            P("dp", "expert", None),
            P("dp", "expert", None),
            P(),
        ),
        out_specs=(
            P("dp", "expert", None),
            P("dp", "expert", None),
            P("dp"),
            P("dp", None),
            P("dp", None),
            P("dp", None),
            P("dp", None),
            P("dp", None),
            P("dp"),
            P("dp", None),
            P("expert", "dp", None),
            P("expert", None, "dp"),
        ),
        check_vma=False,
    )
```
